32 devices in a mesh: rep: 8 (over z, x), tp: 4 (over y, core).
Axes of the slice: x: 2, y: 2, z: 4, core: 2. Of those that a mesh axis runs over, the one named last changes fastest.
Arguments:
- recurrent_state: bfloat16 [64, 128, 64, 256], P('rep', 'tp'), may hold values from -6 to 6
- past_inputs: bfloat16 [64, 3, 8192], P('rep', None, 'tp'), may hold values from -6 to 6
- past_groups: bfloat16 [64, 3, 2048], P('rep'), may hold values from -6 to 6
- anchor_slot: int32 [64], replicated, may hold values from 0 to 63, as said below
- active_counts: int32 [8], replicated, may hold values from 0 to 8, as said below
- new_inputs: bfloat16 [2, 64, 8192], P(None, 'rep', 'tp'), may hold values from -6 to 6
- new_groups: bfloat16 [2, 64, 2048], P(None, 'rep'), may hold values from -6 to 6
- gate_inputs: bfloat16 [2, 64, 8192], P(None, 'rep', 'tp'), may hold values from -24 to 24
- time_steps: float32 [2, 64, 128], P(None, 'rep', 'tp'), may hold values from -6 to 6
- conv_weight: bfloat16 [4, 8192], P(None, 'tp'), may hold values from -3 to 3
- conv_bias: float32 [8192], P('tp'), may hold values from -3 to 3
- group_weight: bfloat16 [4, 2048], replicated, may hold values from -3 to 3
- group_bias: float32 [2048], replicated, may hold values from -3 to 3
- step_bias: float32 [128], P('tp'), may hold values from -3 to -0.5
- decay_log: float32 [128], P('tp'), may hold values from -2.3 to 0
- skip_gain: float32 [128], P('tp'), may hold values from 1 to 4
- norm_gain: float32 [8192], P('tp'), may hold values from 0.5 to 1.5
- out_weight: bfloat16 [8192, 8192], P('tp'), may hold values from -0.0625 to 0.0625
Outputs:
- decoded: bfloat16 [2, 64, 8192], P(None, 'rep', 'tp')
- final_state: bfloat16 [64, 128, 64, 256], P('rep', 'tp')
- final_inputs: bfloat16 [64, 3, 8192], P('rep', None, 'tp')
- final_groups: bfloat16 [64, 3, 2048], P('rep')
The draws below stay inside these ranges and needn't reach their ends.
Inputs may be any that keep to these rules, and one draw needn't show every extreme that they name: `anchor_slot`: slot s of replica r is r * 8 + s; a slot that receives nothing names itself. The replicas fall into two halves, one that may send and one that may receive. A moving request leaves from the last active slots of its source and lands in the slots that follow the receiver's active ones, in order of arrival. No slot is named twice; a sender sends to at most two replicas, a receiver gets from at most two; at most 2 requests go from one replica to another, at most 4 leave or reach one replica. `active_counts`: slots below the count are active; every slot that receives a request is active.
All inputs are finite; a program needn't handle non-finite values.
Results may differ from the reference program's by a relative error of at most 0.0051.
Values may be sent and summed in bfloat16 or wider, within the bound.
A program may use at most 192 MiB of HBM per device.

```python
import math
import jax
import jax.numpy as jnp
from jax import lax

D = 8192
HEADS = 128
HEAD_DIM = 64
STATE = 256
GROUP_HEADS = 32
GROUPS = 4
KERNEL = 4
STEPS = 2
SLOTS = 8
CAP = 2
MOVES = 4
SLOTS_ALL = 64


def plan_tables(key):
    replicas = SLOTS_ALL // SLOTS
    order_key, kept_key, send_key, recv_key = jax.random.split(key, 4)
    placing = jax.random.permutation(order_key, replicas).astype(jnp.int32)
    kept_moves = jax.random.randint(kept_key, (replicas, 2, CAP), 0, 2)
    kept_moves = kept_moves.at[0].set(1).at[replicas - 2].set(1)
    sent_counts = jnp.sum(kept_moves, axis=2).astype(jnp.int32)
    send_base = jax.random.randint(send_key, (replicas,), MOVES, SLOTS + 1).at[0].set(SLOTS)
    recv_base = jax.random.randint(recv_key, (replicas,), 1, SLOTS - MOVES + 1).at[1].set(SLOTS - MOVES)
    anchor = jnp.arange(SLOTS_ALL, dtype=jnp.int32)
    counts = jnp.zeros((replicas,), jnp.int32)
    for position in range(0, replicas, 2):
        counts = counts.at[placing[position]].set(send_base[position] - sent_counts[position, 0] - sent_counts[position, 1])
    for position in range(1, replicas, 2):
        first_sender = position - 1
        second_sender = (position - 3) % replicas
        receive_start = recv_base[position]
        start_first = send_base[first_sender] - sent_counts[first_sender, 0] - sent_counts[first_sender, 1]
        start_second = send_base[second_sender] - sent_counts[second_sender, 1]
        for within in range(CAP):
            target = placing[position] * SLOTS + receive_start + within
            anchor = anchor.at[target].set(jnp.where(within < sent_counts[first_sender, 0], placing[first_sender] * SLOTS + start_first + within, anchor[target]))
            target_two = placing[position] * SLOTS + receive_start + sent_counts[first_sender, 0] + within
            anchor = anchor.at[target_two].set(jnp.where(within < sent_counts[second_sender, 1], placing[second_sender] * SLOTS + start_second + within, anchor[target_two]))
        counts = counts.at[placing[position]].set(receive_start + sent_counts[first_sender, 0] + sent_counts[second_sender, 1])
    return (anchor, counts)


def draw_anchor_slot(key, part):
    anchor, counts = plan_tables(key)
    return anchor


def draw_active_counts(key, part):
    anchor, counts = plan_tables(key)
    return counts


def draw_recurrent_state(key, part):
    key = jax.random.fold_in(key, 23)
    full_shape = (SLOTS_ALL, HEADS, HEAD_DIM, STATE)
    values = jnp.clip(jax.random.normal(key, full_shape, jnp.float32), -6.0, 6.0)
    return values.astype(jnp.bfloat16)


def draw_gate_inputs(key, part):
    key = jax.random.fold_in(key, 11)
    rough_key, scale_key = jax.random.split(key)
    full_shape = (STEPS, SLOTS_ALL, HEADS, HEAD_DIM)
    rough_values = jnp.clip(jax.random.normal(rough_key, full_shape, jnp.float32), -6.0, 6.0)
    head_scale = jnp.exp(jax.random.uniform(scale_key, (STEPS, SLOTS_ALL, HEADS, 1), jnp.float32, math.log(0.25), math.log(4.0)))
    gates = (rough_values * head_scale).reshape(STEPS, SLOTS_ALL, HEADS * HEAD_DIM)
    return gates.astype(jnp.bfloat16)


def shard_levels(own_key, shape, pieces, smallest, high):
    gain, own = 1.0, jax.random.fold_in(own_key, 6)
    for dim, blocks in pieces:
        heights = jnp.exp(jax.random.uniform(jax.random.fold_in(own, dim), (blocks,), jnp.float32, smallest / len(pieces), high / len(pieces)))
        gain = gain * jnp.repeat(heights, shape[dim] // blocks).reshape([-1 if axis == dim else 1 for axis in range(len(shape))])
    return gain


def bell_draw(key, extent, deviation, most, cuts=(), held_as=jnp.bfloat16):
    drawn = jax.random.normal(key, extent, jnp.float32) * deviation
    if len(cuts) > 0:
        drawn = shard_levels(key, extent, cuts, -0.22, 0.18) * drawn
    return jnp.clip(drawn, min=-most, max=most).astype(held_as)


def setup_inputs(seed: int = 0) -> dict:
    key_of = jax.random.split(jax.random.key(seed), 19)
    return {
        "recurrent_state": draw_recurrent_state(jax.random.fold_in(key_of[18], 71), 0),
        "past_inputs": bell_draw(key_of[1], (SLOTS_ALL, KERNEL - 1, HEADS * HEAD_DIM), 1.0, 6.0, ((0, 8), (2, 4))),
        "past_groups": bell_draw(key_of[2], (SLOTS_ALL, KERNEL - 1, GROUPS * 2 * STATE), 1.0, 6.0, ((0, 8),)),
        "anchor_slot": draw_anchor_slot(jax.random.fold_in(key_of[18], 71), 0),
        "active_counts": draw_active_counts(jax.random.fold_in(key_of[18], 71), 0),
        "new_inputs": bell_draw(key_of[5], (STEPS, SLOTS_ALL, HEADS * HEAD_DIM), 1.0, 6.0, ((1, 8), (2, 4))),
        "new_groups": bell_draw(key_of[6], (STEPS, SLOTS_ALL, GROUPS * 2 * STATE), 1.0, 6.0, ((1, 8),)),
        "gate_inputs": draw_gate_inputs(jax.random.fold_in(key_of[18], 71), 0),
        "time_steps": bell_draw(key_of[8], (STEPS, SLOTS_ALL, HEADS), 1.0, 6.0, ((1, 8), (2, 4)), jnp.float32),
        "conv_weight": bell_draw(key_of[9], (KERNEL, HEADS * HEAD_DIM), KERNEL ** -0.5, 3.0, ((1, 4),)),
        "conv_bias": bell_draw(key_of[10], (HEADS * HEAD_DIM,), 0.5, 3.0, ((0, 4),), jnp.float32),
        "group_weight": bell_draw(key_of[11], (KERNEL, GROUPS * 2 * STATE), KERNEL ** -0.5, 3.0),
        "group_bias": bell_draw(key_of[12], (GROUPS * 2 * STATE,), 0.5, 3.0, (), jnp.float32),
        "step_bias": jnp.clip(-3.0 + 2.5 * jax.random.uniform(key_of[13], (HEADS,), jnp.float32) ** shard_levels(key_of[13], (HEADS,), ((0, 4),), -0.2, 0.2), -3.0, -0.5),
        "decay_log": jnp.clip(-2.3 + 2.3 * jax.random.uniform(key_of[14], (HEADS,), jnp.float32) ** shard_levels(key_of[14], (HEADS,), ((0, 4),), -0.2, 0.2), -2.3, 0.0),
        "skip_gain": jnp.clip(1.0 + 3.0 * jax.random.uniform(key_of[15], (HEADS,), jnp.float32) ** shard_levels(key_of[15], (HEADS,), ((0, 4),), -0.2, 0.2), 1.0, 4.0),
        "norm_gain": jnp.clip(1.0 + 0.1 * jax.random.normal(key_of[16], (HEADS * HEAD_DIM,), jnp.float32), 0.5, 1.5),
        "out_weight": bell_draw(key_of[17], (HEADS * HEAD_DIM, D), (HEADS * HEAD_DIM) ** -0.5, 0.0625, ((0, 4),)),
    }


epsilon = 1e-05

def convolve(window, weight, bias):
    return jax.nn.silu(lax.optimization_barrier(jnp.sum(window.astype(jnp.float32) * weight.astype(jnp.float32)[None], axis=1)) + bias)

def reference(recurrent_state, past_inputs, past_groups, anchor_slot, active_counts, new_inputs, new_groups, gate_inputs, time_steps, conv_weight, conv_bias, group_weight, group_bias, step_bias, decay_log, skip_gain, norm_gain, out_weight):
    replicas = SLOTS_ALL // SLOTS
    head_groups = jnp.arange(HEADS, dtype=jnp.int32) // GROUP_HEADS
    decay_rate = jnp.exp(decay_log)

    def one_replica(replica):
        first_slot = (replica * SLOTS).astype(jnp.int32)
        source_rows = lax.dynamic_slice_in_dim(anchor_slot, first_slot, SLOTS)
        state_now = recurrent_state[source_rows].astype(jnp.float32)
        inputs_now = past_inputs[source_rows]
        groups_now = past_groups[source_rows]
        active = jnp.arange(SLOTS, dtype=jnp.int32) < active_counts[replica]
        step_outputs = []
        for step_index in range(STEPS):
            fresh_inputs = lax.dynamic_slice_in_dim(new_inputs[step_index], first_slot, SLOTS)
            fresh_groups = lax.dynamic_slice_in_dim(new_groups[step_index], first_slot, SLOTS)
            fresh_gates = lax.dynamic_slice_in_dim(gate_inputs[step_index], first_slot, SLOTS)
            fresh_steps = lax.dynamic_slice_in_dim(time_steps[step_index], first_slot, SLOTS)
            window = jnp.concatenate([inputs_now, fresh_inputs[:, None, :]], axis=1)
            mixed_inputs = convolve(window, conv_weight, conv_bias).reshape(SLOTS, HEADS, HEAD_DIM)
            inputs_now = window[:, 1:]
            group_window = jnp.concatenate([groups_now, fresh_groups[:, None, :]], axis=1)
            group_mixed = convolve(group_window, group_weight, group_bias).reshape(SLOTS, GROUPS, 2, STATE)
            groups_now = group_window[:, 1:]
            input_head = group_mixed[:, head_groups, 0]
            output_head = group_mixed[:, head_groups, 1]
            step_size = jax.nn.softplus(fresh_steps + step_bias)
            decay_factor = jnp.exp(-step_size * decay_rate)
            state_now = decay_factor[:, :, None, None] * state_now + (step_size[:, :, None] * mixed_inputs)[:, :, :, None] * input_head[:, :, None, :]
            readout = lax.optimization_barrier(jnp.sum(state_now * output_head[:, :, None, :], axis=3)) + skip_gain[None, :, None] * mixed_inputs
            gated_out = (readout * jax.nn.silu(fresh_gates.astype(jnp.float32)).reshape(SLOTS, HEADS, HEAD_DIM)).reshape(SLOTS, HEADS * HEAD_DIM)
            inverse_rms = lax.rsqrt(lax.optimization_barrier(jnp.mean(gated_out * gated_out, axis=1, keepdims=True)) + epsilon)
            normed = (gated_out * inverse_rms * norm_gain).astype(jnp.bfloat16)
            projected = jnp.dot(normed, out_weight, preferred_element_type=jnp.float32)
            step_outputs.append(jnp.where(active[:, None], projected, 0.0).astype(jnp.bfloat16))
        final_state = jnp.where(active[:, None, None, None], state_now, 0.0).astype(jnp.bfloat16)
        final_inputs = jnp.where(active[:, None, None], inputs_now, jnp.zeros_like(inputs_now))
        final_groups = jnp.where(active[:, None, None], groups_now, jnp.zeros_like(groups_now))
        return (jnp.stack(step_outputs), final_state, final_inputs, final_groups)
    results = lax.map(one_replica, jnp.arange(replicas, dtype=jnp.int32))
    decoded = jnp.transpose(results[0], (1, 0, 2, 3)).reshape(STEPS, SLOTS_ALL, D)
    final_state = results[1].reshape(SLOTS_ALL, HEADS, HEAD_DIM, STATE)
    final_inputs = results[2].reshape(SLOTS_ALL, KERNEL - 1, HEADS * HEAD_DIM)
    final_groups = results[3].reshape(SLOTS_ALL, KERNEL - 1, GROUPS * 2 * STATE)
    return (decoded, final_state, final_inputs, final_groups)
```

```python
import functools

import jax
import jax.numpy as jnp
from jax import lax
from jax.sharding import PartitionSpec as P

HEADS = 128
HEAD_DIM = 64
STATE = 256
GROUP_HEADS = 32
GROUPS = 4
STEPS = 2
MOVES = 4


epsilon = 1e-05


def convolve(window, weight, bias):
    return jax.nn.silu(
        jnp.sum(window.astype(jnp.float32) * weight.astype(jnp.float32)[None], axis=1) + bias
    )


def body(
    recurrent_state,
    past_inputs,
    past_groups,
    anchor_slot,
    active_counts,
    new_inputs,
    new_groups,
    gate_inputs,
    time_steps,
    conv_weight,
    conv_bias,
    group_weight,
    group_bias,
    step_bias,
    decay_log,
    skip_gain,
    norm_gain,
    out_weight,
):
    slot_count = recurrent_state.shape[0]
    head_count = recurrent_state.shape[1]
    own_replica = lax.axis_index("rep")
    every_slot = anchor_slot.shape[0]
    relocated = anchor_slot != jnp.arange(every_slot, dtype=jnp.int32)
    source_replica = anchor_slot // slot_count
    source_slot = anchor_slot % slot_count
    own_moved = (
        lax.dynamic_slice_in_dim(relocated.astype(jnp.int32), own_replica * slot_count, slot_count)
        > 0
    )
    local_slots = jnp.arange(slot_count, dtype=jnp.int32)
    replica_count = every_slot // slot_count
    slot_ids = jnp.arange(every_slot, dtype=jnp.int32)
    target_replica = slot_ids // slot_count
    both = relocated[:, None] & relocated[None, :]
    same_sender = both & (source_replica[:, None] == source_replica[None, :])
    same_target = both & (target_replica[:, None] == target_replica[None, :])
    earlier = source_slot[None, :] < source_slot[:, None]
    within = jnp.sum((same_sender & same_target & earlier).astype(jnp.int32), axis=1)
    second = jnp.any(same_sender & ~same_target & earlier, axis=1).astype(jnp.int32)
    arrival = jnp.sum((same_target & (slot_ids[None, :] < slot_ids[:, None])).astype(jnp.int32), axis=1)
    order_key = jnp.where(
        relocated, (second * slot_count + within) * every_slot + slot_ids, 1 << 24
    )
    order = jnp.sum((order_key[None, :] < order_key[:, None]).astype(jnp.int32), axis=1)
    move_limit = max(replica_count // 2, 1) * MOVES
    chosen = relocated[None, :] & (
        order[None, :] == jnp.arange(move_limit, dtype=jnp.int32)[:, None]
    )
    pair_ids = source_replica * (replica_count - 1) + target_replica - (
        target_replica > source_replica
    ).astype(jnp.int32)

    def listed(values):
        return jnp.sum(jnp.where(chosen, values[None, :], 0), axis=1)

    landing = jnp.where(target_replica == own_replica, arrival, MOVES)
    move_pair = listed(pair_ids)
    move_slot = listed(source_slot)
    move_landing = listed(landing)
    move_count = jnp.sum(relocated.astype(jnp.int32))

    channel_rows = recurrent_state.shape[1] * HEAD_DIM
    flat_state = recurrent_state.reshape(slot_count, channel_rows, STATE)
    input_rows = past_inputs.shape[1] * past_inputs.shape[2] // STATE
    group_rows = past_groups.shape[1] * past_groups.shape[2] // STATE
    flat_rows = jnp.concatenate(
        [
            past_inputs.reshape(slot_count, input_rows, STATE),
            past_groups.reshape(slot_count, group_rows, STATE),
        ],
        axis=1,
    )
    branches = [
        functools.partial(lax.ppermute, axis_name="rep", perm=((source, target),))
        for source in range(replica_count)
        for target in range(replica_count)
        if source != target
    ]

    def one_move(index, inbox):
        parcel = jnp.concatenate(
            [
                lax.dynamic_index_in_dim(flat_state, move_slot[index], 0),
                lax.dynamic_index_in_dim(flat_rows, move_slot[index], 0),
            ],
            axis=1,
        )
        got = lax.switch(move_pair[index], branches, parcel)
        return lax.dynamic_update_slice_in_dim(inbox, got, move_landing[index], 0)

    inbox = lax.fori_loop(
        0,
        move_count,
        one_move,
        jnp.zeros((MOVES + 1, channel_rows + input_rows + group_rows, STATE), jnp.bfloat16),
    )
    own_arrival = lax.dynamic_slice_in_dim(arrival, own_replica * slot_count, slot_count)
    lookup = jnp.where(own_moved, own_arrival, MOVES)
    fetched_state = jnp.take(inbox[:, :channel_rows], lookup, axis=0).reshape(recurrent_state.shape)
    fetched_rows = jnp.take(inbox[:, channel_rows:], lookup, axis=0)
    state_now = jnp.where(
        own_moved[:, None, None, None], fetched_state, recurrent_state
    ).astype(jnp.float32)
    rows_now = jnp.where(own_moved[:, None, None], fetched_rows, flat_rows)
    inputs_now = rows_now[:, :input_rows].reshape(past_inputs.shape)
    groups_now = rows_now[:, input_rows:].reshape(past_groups.shape)
    head_ids = lax.axis_index("tp") * head_count + jnp.arange(head_count, dtype=jnp.int32)
    member = (
        head_ids[:, None] // GROUP_HEADS == jnp.arange(GROUPS, dtype=jnp.int32)[None, :]
    ).astype(jnp.float32)
    decay_rate = jnp.exp(decay_log)
    gated_list = []
    for step_index in range(STEPS):
        window = jnp.concatenate([inputs_now, new_inputs[step_index][:, None, :]], axis=1)
        mixed_inputs = convolve(window, conv_weight, conv_bias).reshape(
            slot_count, head_count, HEAD_DIM
        )
        inputs_now = window[:, 1:]
        group_window = jnp.concatenate([groups_now, new_groups[step_index][:, None, :]], axis=1)
        group_mixed = convolve(group_window, group_weight, group_bias).reshape(
            slot_count, GROUPS, 2, STATE
        )
        groups_now = group_window[:, 1:]
        input_head = jnp.sum(group_mixed[:, None, :, 0, :] * member[None, :, :, None], axis=2)
        output_head = jnp.sum(group_mixed[:, None, :, 1, :] * member[None, :, :, None], axis=2)
        step_size = jax.nn.softplus(time_steps[step_index] + step_bias)
        decay_factor = jnp.exp(-step_size * decay_rate)
        state_now = (
            decay_factor[:, :, None, None] * state_now
            + (step_size[:, :, None] * mixed_inputs)[:, :, :, None] * input_head[:, :, None, :]
        )
        readout = (
            jnp.sum(state_now * output_head[:, :, None, :], axis=3)
            + skip_gain[None, :, None] * mixed_inputs
        )
        gated_out = readout * jax.nn.silu(gate_inputs[step_index].astype(jnp.float32)).reshape(
            slot_count, head_count, HEAD_DIM
        )
        gated_list.append(gated_out)
    gated_all = jnp.stack(gated_list)
    partial_value = jnp.sum(gated_all * gated_all, axis=(2, 3))
    totals = lax.psum(partial_value, "tp")
    inverse_rms = lax.rsqrt(totals / (HEADS * HEAD_DIM) + epsilon)
    normed = (
        (gated_all * inverse_rms[:, :, None, None]).reshape(
            STEPS * slot_count, head_count * HEAD_DIM
        )
        * norm_gain
    ).astype(jnp.bfloat16)
    summed = lax.psum_scatter(
        jnp.dot(normed, out_weight, preferred_element_type=jnp.float32).T,
        "tp",
        scatter_dimension=0,
        tiled=True,
    )
    active = local_slots < active_counts[own_replica]
    decoded = summed.T.reshape(STEPS, slot_count, -1)
    decoded = jnp.where(active[None, :, None], decoded, 0.0).astype(jnp.bfloat16)
    final_state = jnp.where(active[:, None, None, None], state_now, 0.0).astype(jnp.bfloat16)
    final_inputs = jnp.where(active[:, None, None], inputs_now, jnp.zeros_like(inputs_now))
    final_groups = jnp.where(active[:, None, None], groups_now, jnp.zeros_like(groups_now))
    return (decoded, final_state, final_inputs, final_groups)


def solution(mesh):
    return jax.shard_map(
        body,
        mesh=mesh,
        in_specs=(
            P("rep", "tp", None, None),
            P("rep", None, "tp"),
            P("rep", None, None),
            P(),
            P(),
            P(None, "rep", "tp"),
            P(None, "rep", None),
            P(None, "rep", "tp"),
            P(None, "rep", "tp"),
            P(None, "tp"),
            P("tp"),
            P(),
            P(),
            P("tp"),
            P("tp"),
            P("tp"),
            P("tp"),
            P("tp", None),
        ),
        out_specs=(
            P(None, "rep", "tp"),
            P("rep", "tp", None, None),
            P("rep", None, "tp"),
            P("rep", None, None),
        ),
        check_vma=False,
    )
```
